256 devices in a mesh: dp: 4 (over z_hi, core), expert: 64 (over x, y, z_lo).
Axes of the slice: x: 4, y: 4, z: 8 (z_hi: 2, z_lo: 4; z = z_hi * 4 + z_lo), core: 2. Of those that a mesh axis runs over, the one named last changes fastest.
Arguments:
- tokens: bfloat16 [65536, 768], P(('dp', 'expert')), may hold values from -6 to 6
- upstream: bfloat16 [65536, 768], P(('dp', 'expert')), may hold values from -4 to 4
- gate_prob: float32 [65536], P(('dp', 'expert')), may hold values from 0.2 to 1
- expert_id: int32 [65536], P(('dp', 'expert')), may hold values from 0 to 63
- slot_index: int32 [65536], P(('dp', 'expert')), may hold values from -1 to 4, as said below
- segment_id: int32 [256, 256], P(('dp', 'expert')), may hold values from 0 to 3, never falling along the last dimension, each value on 1 to 128 neighbouring positions
- weight_in: bfloat16 [64, 3072, 768], P('expert'), may hold values from -0.21875 to 0.21875
- weight_out: bfloat16 [64, 3072, 768], P('expert'), may hold values from -0.109375 to 0.109375
Outputs:
- d_tokens: bfloat16 [65536, 768], P(('dp', 'expert'))
- d_gate: float32 [65536], P(('dp', 'expert'))
- grad_in: bfloat16 [64, 3072, 768], P('expert', 'dp')
- grad_out: bfloat16 [64, 3072, 768], P('expert', 'dp')
The draws below stay inside these ranges and needn't reach their ends.
Inputs may be any that keep to these rules, and one draw needn't show every extreme that they name: `slot_index`: -1 marks a dropped token; otherwise the number of earlier tokens of the same row with the same expert_id. A token is dropped exactly when 5 or more earlier tokens of its row chose its expert. `segment_id`: never falling along a row.
All inputs are finite; a program needn't handle non-finite values.
Results may differ from the reference program's by a relative error of at most 0.02.
Values may be sent and summed in bfloat16 or wider, within the bound.
A program may use at most 128 MiB of HBM per device.

```python
import math
from functools import partial
import jax
import jax.numpy as jnp
import numpy as np
from jax import lax

D = 768
FF = 3072
TOK_DEV = 256
SEGS = 4
EXPERTS = 64
CAP = 5
MOST_SEG = 128
TOKENS = 65536
N_DP = 4
N_EXPERT = 64


def routing_pair(key):
    devices = TOKENS // TOK_DEV
    favored = jax.random.randint(jax.random.fold_in(key, 11), (), 0, EXPERTS)
    spread = jax.random.randint(jax.random.fold_in(key, 12), (devices, TOK_DEV), 0, EXPERTS)
    scores = jax.random.randint(jax.random.fold_in(key, 13), (devices, TOK_DEV), 0, 4096) * TOK_DEV
    scores = scores + jnp.arange(TOK_DEV, dtype=jnp.int32)[None, :]
    order = jnp.argsort(scores, axis=1)
    ranks = jnp.argsort(order, axis=1)
    chosen = jnp.where(ranks < CAP + 1, favored, spread).astype(jnp.int32)
    member = (chosen[:, :, None] == jnp.arange(EXPERTS, dtype=jnp.int32)[None, None, :]).astype(jnp.int32)
    before = jnp.cumsum(member, axis=1) - member
    places = jnp.sum(before * member, axis=2)
    places = jnp.where(places < CAP, places, -1).astype(jnp.int32)
    return (chosen.reshape(TOKENS), places.reshape(TOKENS))


def draw_expert_id(key, part):
    chosen, places = routing_pair(key)
    return chosen


def draw_slot_index(key, part):
    chosen, places = routing_pair(key)
    return places


def block_levels(own_key, shape, pieces, low, top_value):
    gain, own = 1.0, jax.random.fold_in(own_key, 6)
    for dim, blocks in pieces:
        steps = jnp.exp(jax.random.uniform(jax.random.fold_in(own, dim), (blocks,), jnp.float32, low / len(pieces), top_value / len(pieces)))
        gain = gain * jnp.repeat(steps, shape[dim] // blocks).reshape([-1 if axis == dim else 1 for axis in range(len(shape))])
    return gain


def profile(amount, total, most, skew):
    weights = [(1 << 20) // math.isqrt(grade ** skew) + 1 for grade in range(2, amount + 1)]
    rest, holding = total - most - (amount - 1), [1] * (amount - 1)
    while rest > 0:
        candidates = [i for i in range(amount - 1) if holding[i] < most]
        pool, remaining = sum([weights[i] for i in candidates]), rest
        for i in candidates:
            addition = min(most - holding[i], max(1, remaining * weights[i] // pool), rest)
            holding[i] = holding[i] + addition
            rest = rest - addition
    return np.array([most] + holding)


def uneven_parts(key, number_of, total, most, lean):
    if number_of == 2:
        one = jax.random.randint(key, (), max(1, total - most), min(most, total - 1) + 1)
        return jnp.stack([one, total - one])
    tallies = jnp.asarray(profile(number_of, total, most, lean), jnp.int32)
    twos = (number_of - 1) // 2
    source_of, receiver = tallies[1:1 + 2 * twos:2], tallies[2:2 + 2 * twos:2]
    room = jnp.minimum(source_of - 1, most - receiver)
    moved = jax.random.randint(jax.random.fold_in(key, 1), (twos,), 0, 1 << 20) % (room + 1)
    tallies = tallies.at[1:1 + 2 * twos:2].set(source_of - moved).at[2:2 + 2 * twos:2].set(receiver + moved)
    return tallies[jax.random.permutation(jax.random.fold_in(key, 2), number_of)]


def centred(key, extent, scale, reach, split=(), held_as=jnp.bfloat16):
    gain = block_levels(key, extent, split, -0.22, 0.18) if split else 1.0
    array = jax.random.normal(key, extent, jnp.float32) * scale * gain
    return jnp.minimum(jnp.maximum(array, -reach), reach).astype(held_as)


def setup_inputs(seed: int = 0) -> dict:
    key_list = jax.random.split(jax.random.key(seed), 9)
    tokens = centred(key_list[0], (TOKENS, D), 1.0, 6.0, ((0, 256),))
    upstream = centred(key_list[1], (TOKENS, D), 0.3, 4.0, ((0, 256),))
    gate_prob = jnp.clip(0.2 + 0.8 * jax.random.uniform(key_list[2], (TOKENS,), jnp.float32) ** block_levels(key_list[2], (TOKENS,), ((0, 256),), -0.2, 0.2), 0.2, 1.0)
    expert_id = draw_expert_id(jax.random.fold_in(key_list[8], 71), 0)
    slot_index = draw_slot_index(jax.random.fold_in(key_list[8], 71), 0)
    segment_id = jax.vmap(lambda own: jnp.searchsorted(jnp.cumsum(uneven_parts(own, SEGS, TOK_DEV, MOST_SEG, 2)), jnp.arange(TOK_DEV), side="right"))(jax.random.split(key_list[5], (N_DP * N_EXPERT))).reshape((N_DP * N_EXPERT, TOK_DEV)).astype(jnp.int32)
    weight_in = centred(key_list[6], (EXPERTS, FF, D), D ** -0.5, 0.21875, ((0, 64),))
    weight_out = centred(key_list[7], (EXPERTS, FF, D), FF ** -0.5, 0.109375, ((0, 64),))
    return dict(tokens=tokens, upstream=upstream, gate_prob=gate_prob, expert_id=expert_id, slot_index=slot_index, segment_id=segment_id, weight_in=weight_in, weight_out=weight_out)


def gelu_back(pre_act, grad_rows):
    return jax.vjp(partial(jax.nn.gelu, approximate=True), pre_act)[1](grad_rows)[0]

def pick_rows(values, owners):
    padding = jnp.zeros((1,) + values.shape[1:], values.dtype)
    return jnp.concatenate([values, padding], axis=0)[owners]

def reference(tokens, upstream, gate_prob, expert_id, slot_index, segment_id, weight_in, weight_out):
    groups = N_DP
    sources = N_EXPERT
    devices = groups * sources
    slots_all = EXPERTS * CAP
    highest = lax.Precision.HIGHEST
    labels = jnp.arange(SEGS, dtype=jnp.int32)
    member = (segment_id[:, :, None] == labels[None, None, :]).astype(jnp.float32)
    counts = lax.optimization_barrier(jnp.sum(member, axis=1))
    length = lax.optimization_barrier(jnp.sum(member * counts[:, None, :], axis=2))
    doc_weight = TOK_DEV / (SEGS * length)
    upstream_rows = upstream.reshape(devices, TOK_DEV, D).astype(jnp.float32)
    cotangent = (upstream_rows * doc_weight[:, :, None]).astype(jnp.bfloat16)
    token_rows = tokens.reshape(devices, TOK_DEV, D)
    gate_rows = gate_prob.reshape(devices, TOK_DEV)
    route_rows = expert_id.reshape(devices, TOK_DEV)
    place_rows = slot_index.reshape(devices, TOK_DEV)
    position = jnp.where(place_rows >= 0, route_rows * CAP + place_rows, slots_all).astype(jnp.int32)

    def find_owners(place):
        filled = jnp.full((slots_all + 1,), TOK_DEV, jnp.int32)
        return filled.at[place].set(jnp.arange(TOK_DEV, dtype=jnp.int32))[:slots_all]
    owners = jax.vmap(find_owners)(position)

    def arrange(values):
        sent = jax.vmap(pick_rows)(values, owners)
        sent = sent.reshape((groups, sources, EXPERTS, CAP) + values.shape[2:])
        return jnp.moveaxis(sent, 2, 0)
    x_rows = arrange(token_rows)
    c_rows = arrange(cotangent)
    g_rows = arrange(gate_rows)

    def per_expert(operands):
        x_part, c_part, g_part, w_first, w_second = operands
        x_float = x_part.astype(jnp.float32)
        c_float = c_part.astype(jnp.float32)
        first_float = w_first.astype(jnp.float32)
        second_float = w_second.astype(jnp.float32)
        pre_act = jnp.einsum('gskd,fd->gskf', x_float, first_float, precision=highest)
        hidden = jax.nn.gelu(pre_act, approximate=True).astype(jnp.bfloat16)
        hidden_float = hidden.astype(jnp.float32)
        produced = jnp.einsum('gskf,fd->gskd', hidden_float, second_float, precision=highest)
        d_gate_rows = lax.optimization_barrier(jnp.sum(produced * c_float, axis=3))
        d_out = (g_part[..., None] * c_float).astype(jnp.bfloat16)
        d_out_float = d_out.astype(jnp.float32)
        d_hidden = jnp.einsum('gskd,fd->gskf', d_out_float, second_float, precision=highest)
        d_pre = gelu_back(pre_act, d_hidden).astype(jnp.bfloat16)
        d_pre_float = d_pre.astype(jnp.float32)
        d_in_rows = jnp.einsum('gskf,fd->gskd', d_pre_float, first_float, precision=highest).astype(jnp.bfloat16)
        grad_second = jnp.einsum('gskf,gskd->fd', hidden_float, d_out_float, precision=highest).astype(jnp.bfloat16)
        grad_first = jnp.einsum('gskf,gskd->fd', d_pre_float, x_float, precision=highest).astype(jnp.bfloat16)
        return (d_in_rows, d_gate_rows, grad_first, grad_second)
    d_in_rows, d_gate_rows, grad_in, grad_out = lax.map(per_expert, (x_rows, c_rows, g_rows, weight_in, weight_out))

    def send_back(values):
        moved = jnp.moveaxis(values, 0, 2).reshape((devices, slots_all) + values.shape[4:])
        return jax.vmap(pick_rows)(moved, position)
    d_tokens = send_back(d_in_rows).reshape(TOKENS, D)
    d_gate = send_back(d_gate_rows).reshape(TOKENS)
    return (d_tokens, d_gate, grad_in, grad_out)
```

```python
from functools import partial

import jax
import jax.numpy as jnp
from jax import lax
from jax.sharding import PartitionSpec as P

SEGS = 4
BF = jnp.bfloat16
F32 = jnp.float32


def gelu_back(pre_act, grad_rows):
    return jax.vjp(partial(jax.nn.gelu, approximate=True), pre_act)[1](grad_rows)[0]


def mm(spec, a, b):
    return jnp.einsum(spec, a, b, preferred_element_type=F32)


def body(tokens, upstream, gate_prob, expert_id, slot_index, segment_id, weight_in, weight_out):
    experts = lax.axis_size("expert")
    groups = lax.axis_size("dp")
    tok_rows, width = tokens.shape
    hidden_units = weight_in.shape[1]
    capacity = 5 * tok_rows // (4 * experts)
    slots_all = experts * capacity
    own_units = hidden_units // groups
    w_in = weight_in[0]
    w_out = weight_out[0]
    labels = jnp.arange(SEGS, dtype=jnp.int32)
    member = (segment_id[0][:, None] == labels[None, :]).astype(F32)
    counts = jnp.sum(member, axis=0)
    length = jnp.sum(member * counts[None, :], axis=1)
    doc_weight = tok_rows / (SEGS * length)
    cotangent = (upstream.astype(F32) * doc_weight[:, None]).astype(BF)
    d_out_tok = (gate_prob[:, None] * cotangent.astype(F32)).astype(BF)
    position = jnp.where(slot_index >= 0, expert_id * capacity + slot_index, slots_all)
    one_hot = (position[None, :] == jnp.arange(slots_all, dtype=jnp.int32)[:, None]).astype(BF)
    both = jnp.concatenate([tokens, d_out_tok], axis=1)
    sent = mm("st,td->sd", one_hot, both).astype(BF)
    sent = sent.reshape(experts, capacity * 2 * width // 256, 256)
    got = lax.all_to_all(sent, "expert", split_axis=0, concat_axis=0, tiled=True)
    rows = got.reshape(slots_all, 2 * width)
    every = lax.all_gather(rows, "dp", axis=0, tiled=True)
    x_own, d_own = rows[:, :width], rows[:, width:]
    pre = mm("rd,fd->rf", x_own, w_in)
    hidden = jax.nn.gelu(pre, approximate=True).astype(BF)
    d_hidden = mm("rd,fd->rf", d_own, w_out)
    gate_sum = jnp.sum(hidden.astype(F32) * d_hidden, axis=1)
    d_pre = gelu_back(pre, d_hidden).astype(BF)
    d_in = mm("rf,fd->rd", d_pre, w_in).astype(BF)
    gate_high = gate_sum.astype(BF)
    gate_low = (gate_sum - gate_high.astype(F32)).astype(BF)
    gates = jnp.concatenate(
        [
            gate_high.reshape(experts, 1, capacity),
            gate_low.reshape(experts, 1, capacity),
            jnp.zeros((experts, 1, 256 - 2 * capacity), BF),
        ],
        axis=2,
    )
    back = jnp.concatenate([d_in.reshape(experts, capacity * width // 256, 256), gates], axis=1)
    returned = lax.all_to_all(back, "expert", split_axis=0, concat_axis=0, tiled=True)
    back_rows = returned[:, :-1].reshape(slots_all, width)
    back_high = returned[:, -1, :capacity].astype(F32).reshape(slots_all)
    back_low = returned[:, -1, capacity : 2 * capacity].astype(F32).reshape(slots_all)
    d_tokens = mm("st,sd->td", one_hot, back_rows).astype(BF)
    hot = one_hot.astype(F32)
    d_gate = jnp.sum(hot * (back_high + back_low)[:, None], axis=0) / gate_prob
    start = lax.axis_index("dp") * own_units
    w_in_q = lax.dynamic_slice_in_dim(w_in, start, own_units, 0)
    w_out_q = lax.dynamic_slice_in_dim(w_out, start, own_units, 0)
    x_all, d_all = every[:, :width], every[:, width:]
    pre_q = mm("rd,fd->rf", x_all, w_in_q)
    hidden_q = jax.nn.gelu(pre_q, approximate=True).astype(BF)
    d_pre_q = gelu_back(pre_q, mm("rd,fd->rf", d_all, w_out_q)).astype(BF)
    grad_in = mm("rf,rd->fd", d_pre_q, x_all).astype(BF)
    grad_out = mm("rf,rd->fd", hidden_q, d_all).astype(BF)
    return (d_tokens, d_gate, grad_in[None], grad_out[None])


def solution(mesh):
    in_specs = (
        P(("dp", "expert"), None),
        P(("dp", "expert"), None),
        P(("dp", "expert")),
        P(("dp", "expert")),
        P(("dp", "expert")),
        P(("dp", "expert"), None),
        P("expert", None, None),
        P("expert", None, None),
    )
    out_specs = (
        P(("dp", "expert"), None),
        P(("dp", "expert")),
        P("expert", "dp", None),
        P("expert", "dp", None),
    )
    return jax.shard_map(body, mesh=mesh, in_specs=in_specs, out_specs=out_specs, check_vma=False)
```

```python
import math
from functools import partial

import jax
import jax.numpy as jnp
from jax import lax
from jax.experimental import pallas as pl
from jax.experimental.pallas import tpu as pltpu
from jax.sharding import PartitionSpec as P

SEGS = 4
BF = jnp.bfloat16
F32 = jnp.float32
I32 = jnp.int32
MESH = pl.DeviceIdType.MESH
D = 768
FF = 3072
T = 256
E = 64
CAP = 5
W = 256
ROWS = E * CAP
BLK = 16
GRP = 16
GROUPS = E // GRP
GR = GRP * CAP
FQ = FF // 4
FC = 256


def nn(a, b):
    return lax.dot_general(a, b, (((1,), (0,)), ((), ())), preferred_element_type=F32)


def nt(a, b):
    return lax.dot_general(a, b, (((1,), (1,)), ((), ())), preferred_element_type=F32)


def gelu_pair(v):
    scale = math.sqrt(2.0 / math.pi)
    square = v * v
    t = jnp.tanh(scale * (v + 0.044715 * (square * v)))
    half = 0.5 * (1.0 + t)
    slope = half + 0.5 * v * (1.0 - t * t) * (scale * (1.0 + 0.134145 * square))
    return v * half, slope


def iota(shape, dim):
    return lax.broadcasted_iota(I32, shape, dim)


def ones_where(cond):
    return jnp.where(cond, 1.0, 0.0).astype(BF)


def kernel(
    tok_ref, up_ref, gate_ref, exp_ref, slot_ref, seg_ref, win_hbm, wout_hbm,
    dtok_ref, dgate_ref, gin_ref, gout_ref,
    win, wout, packed, near, far, rows, back, ret, acc, gate_acc, gin_acc, gout_acc, unpack,
    w_sem, near_send, far_send, ret_send, near_sem, far_sem, ret_sem, fwd_send, fwd_sem,
):
    dp = lax.axis_index("dp")
    ex = lax.axis_index("expert")
    half = dp // 2
    core = dp % 2
    zl = ex % 4
    z = 4 * half + zl

    win_copy = pltpu.make_async_copy(win_hbm.at[0], win, w_sem.at[0])
    wout_copy = pltpu.make_async_copy(wout_hbm.at[0], wout, w_sem.at[1])
    win_copy.start()
    wout_copy.start()

    barrier = pltpu.get_barrier_semaphore()

    def greet(i, carry):
        e = (ex + i) % E
        for other in range(2):
            @pl.when((i > 0) | (other != half))
            def _():
                pl.semaphore_signal(
                    barrier, inc=1, device_id={"dp": other * 2 + core, "expert": e}, device_id_type=MESH
                )
        return carry

    pl.semaphore_signal(
        barrier, inc=1, device_id={"dp": half * 2 + 1 - core, "expert": ex}, device_id_type=MESH
    )
    lax.fori_loop(0, E, greet, 0)

    seg = seg_ref[...]
    weight = jnp.zeros((1, T), F32)
    for label in range(SEGS):
        same = seg == label
        length = jnp.sum(jnp.where(same, 1.0, 0.0), axis=1, keepdims=True)
        weight = weight + jnp.where(same, T / (SEGS * jnp.maximum(length, 1.0)), 0.0)
    gate = gate_ref[...]
    slot = slot_ref[...]
    kept = slot >= 0
    relative = (exp_ref[...] - ex + E) & (E - 1)
    code = jnp.where(kept, relative * BLK + slot, -4096)
    diagonal = iota((T, T), 0) == iota((T, T), 1)

    def column(row):
        return jnp.sum(jnp.where(diagonal, jnp.broadcast_to(row, (T, T)), 0.0), axis=1, keepdims=True)

    cotangent = (up_ref[...].astype(F32) * column(weight)).astype(BF)
    d_out = (cotangent.astype(F32) * column(gate)).astype(BF)
    tokens = tok_ref[...]
    for g in range(GROUPS):
        place = iota((GRP * BLK, T), 0) + g * GRP * BLK
        x_sum = jnp.zeros((GRP * BLK, W), F32)
        c_sum = jnp.zeros((GRP * BLK, W), F32)
        for k in range(D // W):
            hot = ones_where(place - CAP * k == code)
            x_sum = x_sum + nn(hot, tokens[:, k * W : (k + 1) * W])
            c_sum = c_sum + nn(hot, d_out[:, k * W : (k + 1) * W])
        packed[g * GRP : (g + 1) * GRP, :, 0:W] = x_sum.astype(BF).reshape(GRP, BLK, W)
        packed[g * GRP : (g + 1) * GRP, :, W : 2 * W] = c_sum.astype(BF).reshape(GRP, BLK, W)
    near[0] = packed[0]

    pl.semaphore_wait(barrier, 128)

    def near_half(step):
        hop = jnp.where(step == 2, 2 + 4 * core, jnp.where(step == 3, 7, step))
        return ((z + hop) % 8) // 4

    def send_near(i, carry):
        e = (ex + i) % E
        there = near_half((e % 4 - zl + 4) % 4)
        pltpu.make_async_remote_copy(
            src_ref=packed.at[i], dst_ref=near.at[i], send_sem=near_send, recv_sem=near_sem.at[i // GRP],
            device_id={"dp": there * 2 + core, "expert": e}, device_id_type=MESH,
        ).start()
        return carry

    def send_far(i, carry):
        e = (ex + i) % E
        there = 1 - near_half((e % 4 - zl + 4) % 4)
        pltpu.make_async_remote_copy(
            src_ref=packed.at[i], dst_ref=far.at[i], send_sem=far_send, recv_sem=far_sem.at[i // GRP],
            device_id={"dp": there * 2 + core, "expert": e}, device_id_type=MESH,
        ).start()
        return carry

    lax.fori_loop(1, E, send_near, 0)
    lax.fori_loop(0, E, send_far, 0)

    spot = iota((GR, GRP * BLK), 0)
    spot = spot + 11 * ((spot * 205) >> 10)
    for k in range(D // W):
        unpack[k * GR : (k + 1) * GR, :] = ones_where(iota((GR, GRP * BLK), 1) - CAP * k == spot)

    def take(block, base):
        out = nn(unpack[...], block).astype(BF)
        for k in range(D // W):
            rows[pl.ds(base, GR), k * W : (k + 1) * W] = out[k * GR : (k + 1) * GR, 0:W]
            rows[pl.ds(base, GR), D + k * W : D + (k + 1) * W] = out[k * GR : (k + 1) * GR, W : 2 * W]

    def forward(base, index):
        return pltpu.make_async_remote_copy(
            src_ref=rows.at[pl.ds(base, GR)], dst_ref=rows.at[pl.ds(base, GR)],
            send_sem=fwd_send.at[index], recv_sem=fwd_sem.at[index],
            device_id={"dp": half * 2 + 1 - core, "expert": ex}, device_id_type=MESH,
        )

    forwards = []
    own = pl.multiple_of(core * ROWS, BLK)
    for g in range(GROUPS):
        low = 1 if g == 0 else g * GRP
        part = near.at[pl.ds(low, (g + 1) * GRP - low)]
        pltpu.make_async_copy(part, part, near_sem.at[g]).wait()
        base = pl.multiple_of(own + g * GR, BLK)
        take(near[g * GRP : (g + 1) * GRP].reshape(GRP * BLK, 2 * W), base)
        copy = forward(base, g)
        copy.start()
        forwards.append(copy)

    win_copy.wait()
    wout_copy.wait()
    acc[...] = jnp.zeros_like(acc)
    gate_acc[...] = jnp.zeros_like(gate_acc)

    def near_step(j, carry):
        units = pl.ds(pl.multiple_of(j * FC, FC), FC)
        mine = pl.ds(own, ROWS)
        pre = nt(rows[mine, 0:D], win[units, :])
        d_hidden = nt(rows[mine, D : 2 * D], wout[units, :])
        hidden, slope = gelu_pair(pre)
        gate_acc[...] += hidden.astype(BF).astype(F32) * d_hidden
        acc[...] += nn((d_hidden * slope).astype(BF), win[units, :])
        return carry

    lax.fori_loop(0, FF // FC, near_step, 0)

    spot = iota((GRP * BLK, GR), 1)
    source = (spot * 205) >> 10
    put = iota((GRP * BLK, GR), 0)
    lane = iota((GR, W), 1)
    here = iota((GR, W), 0)
    here = here - CAP * ((here * 205) >> 10)
    for g in range(GROUPS):
        sums = jnp.sum(gate_acc[g * GR : (g + 1) * GR, :], axis=1, keepdims=True)
        high = sums.astype(BF).astype(F32)
        parts = jnp.where(lane == here, high, jnp.where(lane == here + 128, sums - high, 0.0)).astype(BF)
        out = nn(ones_where(put == source * BLK + BLK - 1), parts)
        for k in range(D // W):
            hot = ones_where(put == spot + 11 * source + CAP * k)
            out = out + nn(hot, acc[g * GR : (g + 1) * GR, k * W : (k + 1) * W].astype(BF))
        back[g * GRP : (g + 1) * GRP] = out.astype(BF).reshape(GRP, BLK, W)
    ret[0] = back[0]

    def send_back(i, carry):
        e = (ex - i + E) % E
        step = (zl - e % 4 + 4) % 4
        hop = jnp.where(step == 2, 2 + 4 * core, jnp.where(step == 3, 7, step))
        there = ((z - hop + 8) % 8) // 4
        pltpu.make_async_remote_copy(
            src_ref=back.at[i], dst_ref=ret.at[i], send_sem=ret_send, recv_sem=ret_sem,
            device_id={"dp": there * 2 + core, "expert": e}, device_id_type=MESH,
        ).start()
        return carry

    lax.fori_loop(1, E, send_back, 0)

    def grads(base, count, first, last):
        def step(j, carry):
            units = pl.ds(pl.multiple_of(dp * FQ + j * FC, FC), FC)
            out = pl.ds(pl.multiple_of(j * FC, FC), FC)
            x = rows[base : base + count, 0:D]
            c = rows[base : base + count, D : 2 * D]
            hidden, slope = gelu_pair(nt(win[units, :], x))
            d_pre = (nt(wout[units, :], c) * slope).astype(BF)
            g_in = nn(d_pre, x)
            g_out = nn(hidden.astype(BF), c)
            if not first:
                g_in = g_in + gin_acc[out, :]
                g_out = g_out + gout_acc[out, :]
            if last:
                gin_ref[0, out, :] = g_in.astype(BF)
                gout_ref[0, out, :] = g_out.astype(BF)
            else:
                gin_acc[out, :] = g_in
                gout_acc[out, :] = g_out
            return carry

        lax.fori_loop(0, FQ // FC, step, 0)

    for g in range(GROUPS):
        forwards[g].wait_recv()
    grads(0, 2 * ROWS, True, False)

    def take_far(g):
        part = far.at[pl.ds(g * GRP, GRP)]
        pltpu.make_async_copy(part, part, far_sem.at[g]).wait()
        base = pl.multiple_of(2 * ROWS + 2 * g * GR + core * GR, BLK)
        take(far[g * GRP : (g + 1) * GRP].reshape(GRP * BLK, 2 * W), base)
        copy = forward(base, GROUPS + g)
        copy.start()
        forwards.append(copy)

    take_far(0)
    take_far(1)

    part = ret.at[pl.ds(1, E - 1)]
    pltpu.make_async_copy(part, part, ret_sem).wait()
    returned = ret[...].reshape(E * BLK, W)
    code_column = column(code.astype(F32)).astype(I32)
    place = iota((T, E * BLK), 1)
    for k in range(D // W):
        hot = ones_where(place == code_column + CAP * k)
        dtok_ref[:, k * W : (k + 1) * W] = nn(hot, returned).astype(BF)
    gate_place = column(jnp.where(kept, relative * BLK + BLK - 1, -4096).astype(F32)).astype(I32)
    slot_column = column(slot.astype(F32)).astype(I32)
    picked = nn(ones_where(place == gate_place), returned)
    lane = iota((T, W), 1)
    picked = jnp.where((lane == slot_column) | (lane == slot_column + 128), picked, 0.0)
    sums = jnp.sum(picked, axis=1, keepdims=True)
    sums = jnp.sum(jnp.where(diagonal, jnp.broadcast_to(sums, (T, T)), 0.0), axis=0, keepdims=True)
    dgate_ref[...] = sums / gate

    forwards[GROUPS].wait_recv()
    forwards[GROUPS + 1].wait_recv()
    grads(2 * ROWS, 256, False, False)
    take_far(2)
    take_far(3)
    forwards[GROUPS + 2].wait_recv()
    forwards[GROUPS + 3].wait_recv()
    grads(2 * ROWS + 256, 2 * ROWS - 256, False, True)

    for copy in forwards:
        copy.wait_send()
    part = packed.at[pl.ds(1, E - 1)]
    pltpu.make_async_copy(part, part, near_send).wait()
    pltpu.make_async_copy(packed, packed, far_send).wait()
    part = back.at[pl.ds(1, E - 1)]
    pltpu.make_async_copy(part, part, ret_send).wait()


def body(tokens, upstream, gate_prob, expert_id, slot_index, segment_id, weight_in, weight_out):
    vmem = pl.BlockSpec(memory_space=pltpu.VMEM)
    hbm = pl.BlockSpec(memory_space=pl.ANY)
    dma = pltpu.SemaphoreType.DMA
    d_tokens, d_gate, grad_in, grad_out = pl.pallas_call(
        kernel,
        out_shape=(
            jax.ShapeDtypeStruct((T, D), BF),
            jax.ShapeDtypeStruct((1, T), F32),
            jax.ShapeDtypeStruct((1, FQ, D), BF),
            jax.ShapeDtypeStruct((1, FQ, D), BF),
        ),
        in_specs=[vmem] * 6 + [hbm] * 2,
        out_specs=(vmem, vmem, vmem, vmem),
        scratch_shapes=[
            pltpu.VMEM((FF, D), BF),
            pltpu.VMEM((FF, D), BF),
            pltpu.VMEM((E, BLK, 2 * W), BF),
            pltpu.VMEM((E, BLK, 2 * W), BF),
            pltpu.VMEM((E, BLK, 2 * W), BF),
            pltpu.VMEM((4 * ROWS, 2 * D), BF),
            pltpu.VMEM((E, BLK, W), BF),
            pltpu.VMEM((E, BLK, W), BF),
            pltpu.VMEM((ROWS, D), F32),
            pltpu.VMEM((ROWS, FC), F32),
            pltpu.VMEM((FQ, D), F32),
            pltpu.VMEM((FQ, D), F32),
            pltpu.VMEM((D // W * GR, GRP * BLK), BF),
            dma((2,)),
            dma,
            dma,
            dma,
            dma((GROUPS,)),
            dma((GROUPS,)),
            dma,
            dma((2 * GROUPS,)),
            dma((2 * GROUPS,)),
        ],
        compiler_params=pltpu.CompilerParams(
            collective_id=0, has_side_effects=True, vmem_limit_bytes=52 * 2**20
        ),
    )(
        tokens,
        upstream,
        gate_prob.reshape(1, T),
        expert_id.reshape(1, T),
        slot_index.reshape(1, T),
        segment_id,
        weight_in,
        weight_out,
    )
    return d_tokens, d_gate.reshape(T), grad_in, grad_out


def solution(mesh):
    in_specs = (
        P(("dp", "expert"), None),
        P(("dp", "expert"), None),
        P(("dp", "expert")),
        P(("dp", "expert")),
        P(("dp", "expert")),
        P(("dp", "expert"), None),
        P("expert", None, None),
        P("expert", None, None),
    )
    out_specs = (
        P(("dp", "expert"), None),
        P(("dp", "expert")),
        P("expert", "dp", None),
        P("expert", "dp", None),
    )
    return jax.shard_map(body, mesh=mesh, in_specs=in_specs, out_specs=out_specs, check_vma=False)
```

```python
import math
from functools import partial

import jax
import jax.numpy as jnp
from jax import lax
from jax.experimental import pallas as pl
from jax.experimental.pallas import tpu as pltpu
from jax.sharding import PartitionSpec as P

SEGS = 4
BF = jnp.bfloat16
F32 = jnp.float32
I32 = jnp.int32
MESH = pl.DeviceIdType.MESH
D = 768
FF = 3072
T = 256
E = 64
CAP = 5
W = 256
ROWS = E * CAP
BLK = 16
GRP = 16
GROUPS = E // GRP
GR = GRP * CAP
FQ = FF // 4
FC = 256
LIMIT = 60
FIRST = 28
PACE = 3


def nn(a, b):
    return lax.dot_general(a, b, (((1,), (0,)), ((), ())), preferred_element_type=F32)


def nt(a, b):
    return lax.dot_general(a, b, (((1,), (1,)), ((), ())), preferred_element_type=F32)


def gelu_pair(v):
    scale = math.sqrt(2.0 / math.pi)
    square = v * v
    t = jnp.tanh(scale * (v + 0.044715 * (square * v)))
    half = 0.5 * (1.0 + t)
    slope = half + 0.5 * v * (1.0 - t * t) * (scale * (1.0 + 0.134145 * square))
    return v * half, slope


def iota(shape, dim):
    return lax.broadcasted_iota(I32, shape, dim)


def ones_where(cond):
    return jnp.where(cond, 1.0, 0.0).astype(BF)


def kernel(
    tok_hbm, up_hbm, gate_hbm, exp_hbm, slot_hbm, seg_hbm, win_hbm, wout_hbm,
    dtok_ref, dgate_ref, gin_ref, gout_ref,
    tok_ref, up_ref, gate_ref, exp_ref, slot_ref, seg_ref, win, wout, packed, near, far, rows, back, ret, acc, gate_acc, gin_acc, gout_acc, unpack,
    in_sem, w_sem, ready, near_send, far_send, ret_send, near_sem, far_sem, ret_sem, fwd_send, fwd_sem,
):
    dp = lax.axis_index("dp")
    ex = lax.axis_index("expert")
    half = dp // 2
    core = dp % 2
    zl = ex % 4
    z = 4 * half + zl

    x, y = ex // 16, ex // 4 % 4
    loads = [
        pltpu.make_async_copy(source, target, in_sem.at[index])
        for index, (source, target) in enumerate(
            (
                (up_hbm, up_ref),
                (tok_hbm, tok_ref),
                (seg_hbm, seg_ref),
                (gate_hbm, gate_ref),
                (exp_hbm, exp_ref),
                (slot_hbm, slot_ref),
            )
        )
    ]
    for load in loads:
        load.start()

    def signal(semaphore, group, expert):
        pl.semaphore_signal(semaphore, inc=1, device_id={"dp": group, "expert": expert}, device_id_type=MESH)

    def signal_ring(semaphore):
        for hop in range(1, 8):
            there = (z + hop) % 8
            signal(semaphore, there // 4 * 2 + core, ex - zl + there % 4)

    barrier = pltpu.get_barrier_semaphore()
    signal(barrier, half * 2 + 1 - core, ex)
    for hop in range(1, 16):
        signal(barrier, dp, (x + hop // 4) % 4 * 16 + (y + hop % 4) % 4 * 4 + zl)
    signal_ring(barrier)
    for load in loads:
        load.wait()
    win_copy = pltpu.make_async_copy(win_hbm.at[0], win, w_sem.at[0])
    wout_copy = pltpu.make_async_copy(wout_hbm.at[0], wout, w_sem.at[1])
    win_copy.start()
    wout_copy.start()

    seg = seg_ref[...]
    weight = jnp.zeros((1, T), F32)
    for label in range(SEGS):
        same = seg == label
        length = jnp.sum(jnp.where(same, 1.0, 0.0), axis=1, keepdims=True)
        weight = weight + jnp.where(same, T / (SEGS * jnp.maximum(length, 1.0)), 0.0)
    gate = gate_ref[...]
    slot = slot_ref[...]
    kept = slot >= 0
    relative = (exp_ref[...] - ex + E) & (E - 1)
    code = jnp.where(kept, relative * BLK + slot, -4096)
    diagonal = iota((T, T), 0) == iota((T, T), 1)

    def column(row):
        return jnp.sum(jnp.where(diagonal, jnp.broadcast_to(row, (T, T)), 0.0), axis=1, keepdims=True)

    cotangent = (up_ref[...].astype(F32) * column(weight)).astype(BF)
    d_out = (cotangent.astype(F32) * column(gate)).astype(BF)
    tokens = tok_ref[...]
    pl.semaphore_wait(barrier, 23)
    signal_ring(ready)

    def near_half(step):
        hop = jnp.where(step == 2, 2 + 4 * core, jnp.where(step == 3, 7, step))
        return ((z + hop) % 8) // 4

    def send_near(i, carry):
        e = (ex + i) % E
        there = near_half((e % 4 - zl + 4) % 4)
        pltpu.make_async_remote_copy(
            src_ref=packed.at[i], dst_ref=near.at[i], send_sem=near_send, recv_sem=near_sem.at[i // GRP],
            device_id={"dp": there * 2 + core, "expert": e}, device_id_type=MESH,
        ).start()
        return carry

    def send_far(i, carry):
        e = (ex + i) % E
        there = 1 - near_half((e % 4 - zl + 4) % 4)
        pltpu.make_async_remote_copy(
            src_ref=packed.at[i], dst_ref=far.at[i], send_sem=far_send, recv_sem=far_sem.at[i // GRP],
            device_id={"dp": there * 2 + core, "expert": e}, device_id_type=MESH,
        ).start()
        return carry

    for g in range(GROUPS):
        place = iota((GRP * BLK, T), 0) + g * GRP * BLK
        x_sum = jnp.zeros((GRP * BLK, W), F32)
        c_sum = jnp.zeros((GRP * BLK, W), F32)
        for k in range(D // W):
            hot = ones_where(place - CAP * k == code)
            x_sum = x_sum + nn(hot, tokens[:, k * W : (k + 1) * W])
            c_sum = c_sum + nn(hot, d_out[:, k * W : (k + 1) * W])
        packed[g * GRP : (g + 1) * GRP, :, 0:W] = x_sum.astype(BF).reshape(GRP, BLK, W)
        packed[g * GRP : (g + 1) * GRP, :, W : 2 * W] = c_sum.astype(BF).reshape(GRP, BLK, W)
        if g == 0:
            near[0] = packed[0]
            pl.semaphore_wait(ready, 7)
        lax.fori_loop(max(1, g * GRP), (g + 1) * GRP, send_near, 0)
    lax.fori_loop(0, FIRST, send_far, 0)

    spot = iota((GR, GRP * BLK), 0)
    spot = spot + 11 * ((spot * 205) >> 10)
    for k in range(D // W):
        unpack[k * GR : (k + 1) * GR, :] = ones_where(iota((GR, GRP * BLK), 1) - CAP * k == spot)

    def take(block, base):
        out = nn(unpack[...], block).astype(BF)
        for k in range(D // W):
            rows[pl.ds(base, GR), k * W : (k + 1) * W] = out[k * GR : (k + 1) * GR, 0:W]
            rows[pl.ds(base, GR), D + k * W : D + (k + 1) * W] = out[k * GR : (k + 1) * GR, W : 2 * W]

    def forward(base, index):
        return pltpu.make_async_remote_copy(
            src_ref=rows.at[pl.ds(base, GR)], dst_ref=rows.at[pl.ds(base, GR)],
            send_sem=fwd_send.at[index], recv_sem=fwd_sem.at[index],
            device_id={"dp": half * 2 + 1 - core, "expert": ex}, device_id_type=MESH,
        )

    forwards = []
    own = pl.multiple_of(core * ROWS, BLK)
    for g in range(GROUPS):
        low = 1 if g == 0 else g * GRP
        part = near.at[pl.ds(low, (g + 1) * GRP - low)]
        pltpu.make_async_copy(part, part, near_sem.at[g]).wait()
        base = pl.multiple_of(own + g * GR, BLK)
        take(near[g * GRP : (g + 1) * GRP].reshape(GRP * BLK, 2 * W), base)
        copy = forward(base, g)
        copy.start()
        forwards.append(copy)

    win_copy.wait()
    wout_copy.wait()
    acc[...] = jnp.zeros_like(acc)
    gate_acc[...] = jnp.zeros_like(gate_acc)

    def near_step(j, carry):
        for extra in range(PACE):
            send_far(FIRST + PACE * j + extra, 0)
        units = pl.ds(pl.multiple_of(j * FC, FC), FC)
        mine = pl.ds(own, ROWS)
        pre = nt(rows[mine, 0:D], win[units, :])
        d_hidden = nt(rows[mine, D : 2 * D], wout[units, :])
        hidden, slope = gelu_pair(pre)
        gate_acc[...] += hidden.astype(BF).astype(F32) * d_hidden
        acc[...] += nn((d_hidden * slope).astype(BF), win[units, :])
        return carry

    lax.fori_loop(0, FF // FC, near_step, 0)

    spot = iota((GRP * BLK, GR), 1)
    source = (spot * 205) >> 10
    put = iota((GRP * BLK, GR), 0)
    lane = iota((GR, W), 1)
    here = iota((GR, W), 0)
    here = here - CAP * ((here * 205) >> 10)
    for g in range(GROUPS):
        sums = jnp.sum(gate_acc[g * GR : (g + 1) * GR, :], axis=1, keepdims=True)
        high = sums.astype(BF).astype(F32)
        parts = jnp.where(lane == here, high, jnp.where(lane == here + 128, sums - high, 0.0)).astype(BF)
        out = nn(ones_where(put == source * BLK + BLK - 1), parts)
        for k in range(D // W):
            hot = ones_where(put == spot + 11 * source + CAP * k)
            out = out + nn(hot, acc[g * GR : (g + 1) * GR, k * W : (k + 1) * W].astype(BF))
        back[g * GRP : (g + 1) * GRP] = out.astype(BF).reshape(GRP, BLK, W)
    ret[0] = back[0]

    def send_back(i, carry):
        e = (ex - i + E) % E
        step = (zl - e % 4 + 4) % 4
        hop = jnp.where(step == 2, 2 + 4 * core, jnp.where(step == 3, 7, step))
        there = ((z - hop + 8) % 8) // 4
        pltpu.make_async_remote_copy(
            src_ref=back.at[i], dst_ref=ret.at[i], send_sem=ret_send, recv_sem=ret_sem,
            device_id={"dp": there * 2 + core, "expert": e}, device_id_type=MESH,
        ).start()
        return carry

    lax.fori_loop(1, E, send_back, 0)

    def grads(base, count, first, last):
        def step(j, carry):
            units = pl.ds(pl.multiple_of(dp * FQ + j * FC, FC), FC)
            out = pl.ds(j * FC if last else pl.multiple_of(j * FC, FC), FC)
            x = rows[base : base + count, 0:D]
            c = rows[base : base + count, D : 2 * D]
            hidden, slope = gelu_pair(nt(win[units, :], x))
            d_pre = (nt(wout[units, :], c) * slope).astype(BF)
            g_in = nn(d_pre, x)
            g_out = nn(hidden.astype(BF), c)
            if not first:
                g_in = g_in + gin_acc[out, :]
                g_out = g_out + gout_acc[out, :]
            if last:
                gin_ref[0, out, :] = g_in.astype(BF)
                gout_ref[0, out, :] = g_out.astype(BF)
            else:
                gin_acc[out, :] = g_in
                gout_acc[out, :] = g_out
            return carry

        if last:
            for j in range(FQ // FC):
                step(j, 0)
        else:
            lax.fori_loop(0, FQ // FC, step, 0)

    for g in range(GROUPS):
        forwards[g].wait_recv()
    grads(0, 2 * ROWS, True, False)

    def take_far(g):
        part = far.at[pl.ds(g * GRP, GRP)]
        pltpu.make_async_copy(part, part, far_sem.at[g]).wait()
        base = pl.multiple_of(2 * ROWS + 2 * g * GR + core * GR, BLK)
        take(far[g * GRP : (g + 1) * GRP].reshape(GRP * BLK, 2 * W), base)
        copy = forward(base, GROUPS + g)
        copy.start()
        forwards.append(copy)

    take_far(0)
    take_far(1)

    forwards[GROUPS].wait_recv()
    forwards[GROUPS + 1].wait_recv()
    grads(2 * ROWS, 4 * GR, False, False)
    take_far(2)
    forwards[GROUPS + 2].wait_recv()
    grads(2 * ROWS + 4 * GR, 2 * GR, False, False)
    take_far(3)
    forwards[GROUPS + 3].wait_recv()
    grads(2 * ROWS + 6 * GR, 2 * GR, False, True)

    part = ret.at[pl.ds(1, E - 1)]
    pltpu.make_async_copy(part, part, ret_sem).wait()
    returned = ret[...].reshape(E * BLK, W)
    code_column = column(code.astype(F32)).astype(I32)
    place = iota((T, E * BLK), 1)
    for k in range(D // W):
        hot = ones_where(place == code_column + CAP * k)
        dtok_ref[:, k * W : (k + 1) * W] = nn(hot, returned).astype(BF)
    gate_place = column(jnp.where(kept, relative * BLK + BLK - 1, -4096).astype(F32)).astype(I32)
    slot_column = column(slot.astype(F32)).astype(I32)
    picked = nn(ones_where(place == gate_place), returned)
    lane = iota((T, W), 1)
    picked = jnp.where((lane == slot_column) | (lane == slot_column + 128), picked, 0.0)
    sums = jnp.sum(picked, axis=1, keepdims=True)
    sums = jnp.sum(jnp.where(diagonal, jnp.broadcast_to(sums, (T, T)), 0.0), axis=0, keepdims=True)
    dgate_ref[...] = sums / gate

    for copy in forwards:
        copy.wait_send()
    part = packed.at[pl.ds(1, E - 1)]
    pltpu.make_async_copy(part, part, near_send).wait()
    pltpu.make_async_copy(packed, packed, far_send).wait()
    part = back.at[pl.ds(1, E - 1)]
    pltpu.make_async_copy(part, part, ret_send).wait()


def deliver(*refs):
    sources, targets, stage = refs[:4], refs[4:8], refs[8:12]
    inward, outward = refs[12:]
    loads = [pltpu.make_async_copy(sources[i], stage[i], inward.at[i]) for i in range(4)]
    stores = [pltpu.make_async_copy(stage[i], targets[i], outward.at[i]) for i in range(4)]
    for load in loads:
        load.start()
    for load, store in zip(loads, stores):
        load.wait()
        store.start()
    for store in stores:
        store.wait()


def body(tokens, upstream, gate_prob, expert_id, slot_index, segment_id, weight_in, weight_out):
    vmem = pl.BlockSpec(memory_space=pltpu.VMEM)
    hbm = pl.BlockSpec(memory_space=pl.ANY)
    dma = pltpu.SemaphoreType.DMA
    d_tokens, d_gate, grad_in, grad_out = pl.pallas_call(
        kernel,
        out_shape=(
            jax.ShapeDtypeStruct((T, D), BF),
            jax.ShapeDtypeStruct((1, T), F32),
            jax.ShapeDtypeStruct((1, FQ, D), BF),
            jax.ShapeDtypeStruct((1, FQ, D), BF),
        ),
        in_specs=[hbm] * 8,
        out_specs=(vmem, vmem, vmem, vmem),
        scratch_shapes=[
            pltpu.VMEM((T, D), BF),
            pltpu.VMEM((T, D), BF),
            pltpu.VMEM((1, T), F32),
            pltpu.VMEM((1, T), I32),
            pltpu.VMEM((1, T), I32),
            pltpu.VMEM((1, T), I32),
            pltpu.VMEM((FF, D), BF),
            pltpu.VMEM((FF, D), BF),
            pltpu.VMEM((E, BLK, 2 * W), BF),
            pltpu.VMEM((E, BLK, 2 * W), BF),
            pltpu.VMEM((E, BLK, 2 * W), BF),
            pltpu.VMEM((4 * ROWS, 2 * D), BF),
            pltpu.VMEM((E, BLK, W), BF),
            pltpu.VMEM((E, BLK, W), BF),
            pltpu.VMEM((ROWS, D), F32),
            pltpu.VMEM((ROWS, FC), F32),
            pltpu.VMEM((FQ, D), F32),
            pltpu.VMEM((FQ, D), F32),
            pltpu.VMEM((D // W * GR, GRP * BLK), BF),
            dma((6,)),
            dma((2,)),
            pltpu.SemaphoreType.REGULAR,
            dma,
            dma,
            dma,
            dma((GROUPS,)),
            dma((GROUPS,)),
            dma,
            dma((2 * GROUPS,)),
            dma((2 * GROUPS,)),
        ],
        compiler_params=pltpu.CompilerParams(
            collective_id=0, has_side_effects=True, vmem_limit_bytes=LIMIT * 2**20
        ),
    )(
        tokens,
        upstream,
        gate_prob.reshape(1, T),
        expert_id.reshape(1, T),
        slot_index.reshape(1, T),
        segment_id,
        weight_in,
        weight_out,
    )
    results = (d_tokens, d_gate, grad_in, grad_out)
    d_tokens, d_gate, grad_in, grad_out = pl.pallas_call(
        deliver,
        out_shape=tuple(jax.ShapeDtypeStruct(r.shape, r.dtype) for r in results),
        in_specs=[hbm] * 4,
        out_specs=(hbm,) * 4,
        scratch_shapes=[pltpu.VMEM(r.shape, r.dtype) for r in results] + [dma((4,)), dma((4,))],
    )(*results)
    return d_tokens, d_gate.reshape(T), grad_in, grad_out


def solution(mesh):
    in_specs = (
        P(("dp", "expert"), None),
        P(("dp", "expert"), None),
        P(("dp", "expert")),
        P(("dp", "expert")),
        P(("dp", "expert")),
        P(("dp", "expert"), None),
        P("expert", None, None),
        P("expert", None, None),
    )
    out_specs = (
        P(("dp", "expert"), None),
        P(("dp", "expert")),
        P("expert", "dp", None),
        P("expert", "dp", None),
    )
    return jax.shard_map(body, mesh=mesh, in_specs=in_specs, out_specs=out_specs, check_vma=False)
```

```python
import math
from functools import partial

import jax
import jax.numpy as jnp
from jax import lax
from jax.experimental import pallas as pl
from jax.experimental.pallas import tpu as pltpu
from jax.sharding import PartitionSpec as P

SEGS = 4
BF = jnp.bfloat16
F32 = jnp.float32
I32 = jnp.int32
MESH = pl.DeviceIdType.MESH
D = 768
FF = 3072
T = 256
E = 64
CAP = 5
W = 256
ROWS = E * CAP
BLK = 16
GRP = 16
GROUPS = E // GRP
GR = GRP * CAP
FQ = FF // 4
FC = 256
LIMIT = 60
FIRST = 28
PACE = 3


def nn(a, b):
    return lax.dot_general(a, b, (((1,), (0,)), ((), ())), preferred_element_type=F32)


def nt(a, b):
    return lax.dot_general(a, b, (((1,), (1,)), ((), ())), preferred_element_type=F32)


def gelu_pair(v):
    scale = math.sqrt(2.0 / math.pi)
    square = v * v
    t = jnp.tanh(scale * (v + 0.044715 * (square * v)))
    half = 0.5 * (1.0 + t)
    slope = half + 0.5 * v * (1.0 - t * t) * (scale * (1.0 + 0.134145 * square))
    return v * half, slope


def iota(shape, dim):
    return lax.broadcasted_iota(I32, shape, dim)


def ones_where(cond):
    return jnp.where(cond, 1.0, 0.0).astype(BF)


def column(row):
    diagonal = iota((T, T), 0) == iota((T, T), 1)
    return jnp.sum(jnp.where(diagonal, jnp.broadcast_to(row, (T, T)), 0.0), axis=1, keepdims=True)


def kernel(
    tok_hbm, up_hbm, gate_hbm, exp_hbm, slot_hbm, seg_hbm, win_hbm, wout_hbm,
    ret, gin_out, gout_out,
    tok_ref, up_ref, gate_ref, exp_ref, slot_ref, seg_ref, win, wout, packed, near, far, rows, back, gin_ref, gout_ref, acc, gate_acc, gin_acc, gout_acc, unpack,
    in_sem, w_sem, ready, near_send, far_send, ret_send, near_sem, far_sem, ret_sem, fwd_send, fwd_sem, out_sem,
):
    dp = lax.axis_index("dp")
    ex = lax.axis_index("expert")
    half = dp // 2
    core = dp % 2
    zl = ex % 4
    z = 4 * half + zl

    x, y = ex // 16, ex // 4 % 4
    loads = [
        pltpu.make_async_copy(source, target, in_sem.at[index])
        for index, (source, target) in enumerate(
            (
                (up_hbm, up_ref),
                (tok_hbm, tok_ref),
                (seg_hbm, seg_ref),
                (gate_hbm, gate_ref),
                (exp_hbm, exp_ref),
                (slot_hbm, slot_ref),
            )
        )
    ]
    for load in loads:
        load.start()

    def signal(semaphore, group, expert):
        pl.semaphore_signal(semaphore, inc=1, device_id={"dp": group, "expert": expert}, device_id_type=MESH)

    def signal_ring(semaphore):
        for hop in range(1, 8):
            there = (z + hop) % 8
            signal(semaphore, there // 4 * 2 + core, ex - zl + there % 4)

    barrier = pltpu.get_barrier_semaphore()
    signal(barrier, half * 2 + 1 - core, ex)
    for hop in range(1, 16):
        signal(barrier, dp, (x + hop // 4) % 4 * 16 + (y + hop % 4) % 4 * 4 + zl)
    signal_ring(barrier)
    for load in loads:
        load.wait()
    win_copy = pltpu.make_async_copy(win_hbm.at[0], win, w_sem.at[0])
    wout_copy = pltpu.make_async_copy(wout_hbm.at[0], wout, w_sem.at[1])
    win_copy.start()
    wout_copy.start()

    seg = seg_ref[...]
    weight = jnp.zeros((1, T), F32)
    for label in range(SEGS):
        same = seg == label
        length = jnp.sum(jnp.where(same, 1.0, 0.0), axis=1, keepdims=True)
        weight = weight + jnp.where(same, T / (SEGS * jnp.maximum(length, 1.0)), 0.0)
    gate = gate_ref[...]
    slot = slot_ref[...]
    kept = slot >= 0
    relative = (exp_ref[...] - ex + E) & (E - 1)
    code = jnp.where(kept, relative * BLK + slot, -4096)
    cotangent = (up_ref[...].astype(F32) * column(weight)).astype(BF)
    d_out = (cotangent.astype(F32) * column(gate)).astype(BF)
    tokens = tok_ref[...]
    pl.semaphore_wait(barrier, 23)
    signal_ring(ready)

    def near_half(step):
        hop = jnp.where(step == 2, 2 + 4 * core, jnp.where(step == 3, 7, step))
        return ((z + hop) % 8) // 4

    def send_near(i, carry):
        e = (ex + i) % E
        there = near_half((e % 4 - zl + 4) % 4)
        pltpu.make_async_remote_copy(
            src_ref=packed.at[i], dst_ref=near.at[i], send_sem=near_send, recv_sem=near_sem.at[i // GRP],
            device_id={"dp": there * 2 + core, "expert": e}, device_id_type=MESH,
        ).start()
        return carry

    def send_far(i, carry):
        e = (ex + i) % E
        there = 1 - near_half((e % 4 - zl + 4) % 4)
        pltpu.make_async_remote_copy(
            src_ref=packed.at[i], dst_ref=far.at[i], send_sem=far_send, recv_sem=far_sem.at[i // GRP],
            device_id={"dp": there * 2 + core, "expert": e}, device_id_type=MESH,
        ).start()
        return carry

    for g in range(GROUPS):
        place = iota((GRP * BLK, T), 0) + g * GRP * BLK
        x_sum = jnp.zeros((GRP * BLK, W), F32)
        c_sum = jnp.zeros((GRP * BLK, W), F32)
        for k in range(D // W):
            hot = ones_where(place - CAP * k == code)
            x_sum = x_sum + nn(hot, tokens[:, k * W : (k + 1) * W])
            c_sum = c_sum + nn(hot, d_out[:, k * W : (k + 1) * W])
        packed[g * GRP : (g + 1) * GRP, :, 0:W] = x_sum.astype(BF).reshape(GRP, BLK, W)
        packed[g * GRP : (g + 1) * GRP, :, W : 2 * W] = c_sum.astype(BF).reshape(GRP, BLK, W)
        if g == 0:
            near[0] = packed[0]
            pl.semaphore_wait(ready, 7)
        lax.fori_loop(max(1, g * GRP), (g + 1) * GRP, send_near, 0)
    lax.fori_loop(0, FIRST, send_far, 0)

    spot = iota((GR, GRP * BLK), 0)
    spot = spot + 11 * ((spot * 205) >> 10)
    for k in range(D // W):
        unpack[k * GR : (k + 1) * GR, :] = ones_where(iota((GR, GRP * BLK), 1) - CAP * k == spot)

    def take(block, base):
        out = nn(unpack[...], block).astype(BF)
        for k in range(D // W):
            rows[pl.ds(base, GR), k * W : (k + 1) * W] = out[k * GR : (k + 1) * GR, 0:W]
            rows[pl.ds(base, GR), D + k * W : D + (k + 1) * W] = out[k * GR : (k + 1) * GR, W : 2 * W]

    def forward(base, index):
        return pltpu.make_async_remote_copy(
            src_ref=rows.at[pl.ds(base, GR)], dst_ref=rows.at[pl.ds(base, GR)],
            send_sem=fwd_send.at[index], recv_sem=fwd_sem.at[index],
            device_id={"dp": half * 2 + 1 - core, "expert": ex}, device_id_type=MESH,
        )

    forwards = []
    own = pl.multiple_of(core * ROWS, BLK)
    for g in range(GROUPS):
        low = 1 if g == 0 else g * GRP
        part = near.at[pl.ds(low, (g + 1) * GRP - low)]
        pltpu.make_async_copy(part, part, near_sem.at[g]).wait()
        base = pl.multiple_of(own + g * GR, BLK)
        take(near[g * GRP : (g + 1) * GRP].reshape(GRP * BLK, 2 * W), base)
        copy = forward(base, g)
        copy.start()
        forwards.append(copy)

    win_copy.wait()
    wout_copy.wait()
    acc[...] = jnp.zeros_like(acc)
    gate_acc[...] = jnp.zeros_like(gate_acc)

    def near_step(j, carry):
        for extra in range(PACE):
            send_far(FIRST + PACE * j + extra, 0)
        units = pl.ds(pl.multiple_of(j * FC, FC), FC)
        mine = pl.ds(own, ROWS)
        pre = nt(rows[mine, 0:D], win[units, :])
        d_hidden = nt(rows[mine, D : 2 * D], wout[units, :])
        hidden, slope = gelu_pair(pre)
        gate_acc[...] += hidden.astype(BF).astype(F32) * d_hidden
        acc[...] += nn((d_hidden * slope).astype(BF), win[units, :])
        return carry

    lax.fori_loop(0, FF // FC, near_step, 0)

    spot = iota((GRP * BLK, GR), 1)
    source = (spot * 205) >> 10
    put = iota((GRP * BLK, GR), 0)
    lane = iota((GR, W), 1)
    here = iota((GR, W), 0)
    here = here - CAP * ((here * 205) >> 10)
    for g in range(GROUPS):
        sums = jnp.sum(gate_acc[g * GR : (g + 1) * GR, :], axis=1, keepdims=True)
        high = sums.astype(BF).astype(F32)
        parts = jnp.where(lane == here, high, jnp.where(lane == here + 128, sums - high, 0.0)).astype(BF)
        out = nn(ones_where(put == source * BLK + BLK - 1), parts)
        for k in range(D // W):
            hot = ones_where(put == spot + 11 * source + CAP * k)
            out = out + nn(hot, acc[g * GR : (g + 1) * GR, k * W : (k + 1) * W].astype(BF))
        back[g * GRP : (g + 1) * GRP] = out.astype(BF).reshape(GRP, BLK, W)
    kept_block = pltpu.make_async_copy(back.at[0], ret.at[0], out_sem.at[2 * FQ // FC])
    kept_block.start()

    def send_back(i, carry):
        e = (ex - i + E) % E
        step = (zl - e % 4 + 4) % 4
        hop = jnp.where(step == 2, 2 + 4 * core, jnp.where(step == 3, 7, step))
        there = ((z - hop + 8) % 8) // 4
        pltpu.make_async_remote_copy(
            src_ref=back.at[i], dst_ref=ret.at[i], send_sem=ret_send, recv_sem=ret_sem,
            device_id={"dp": there * 2 + core, "expert": e}, device_id_type=MESH,
        ).start()
        return carry

    lax.fori_loop(1, E, send_back, 0)

    stores = [kept_block]

    def grads(base, count, first, last):
        def step(j, carry):
            units = pl.ds(pl.multiple_of(dp * FQ + j * FC, FC), FC)
            out = pl.ds(j * FC if last else pl.multiple_of(j * FC, FC), FC)
            x = rows[base : base + count, 0:D]
            c = rows[base : base + count, D : 2 * D]
            hidden, slope = gelu_pair(nt(win[units, :], x))
            d_pre = (nt(wout[units, :], c) * slope).astype(BF)
            g_in = nn(d_pre, x)
            g_out = nn(hidden.astype(BF), c)
            if not first:
                g_in = g_in + gin_acc[out, :]
                g_out = g_out + gout_acc[out, :]
            if last:
                gin_ref[out, :] = g_in.astype(BF)
                gout_ref[out, :] = g_out.astype(BF)
                for index, (source, target) in enumerate(((gin_ref, gin_out), (gout_ref, gout_out))):
                    copy = pltpu.make_async_copy(
                        source.at[out], target.at[0, out], out_sem.at[2 * j + index]
                    )
                    copy.start()
                    stores.append(copy)
            else:
                gin_acc[out, :] = g_in
                gout_acc[out, :] = g_out
            return carry

        if last:
            for j in range(FQ // FC):
                step(j, 0)
        else:
            lax.fori_loop(0, FQ // FC, step, 0)

    for g in range(GROUPS):
        forwards[g].wait_recv()
    grads(0, 2 * ROWS, True, False)

    def take_far(g):
        part = far.at[pl.ds(g * GRP, GRP)]
        pltpu.make_async_copy(part, part, far_sem.at[g]).wait()
        base = pl.multiple_of(2 * ROWS + 2 * g * GR + core * GR, BLK)
        take(far[g * GRP : (g + 1) * GRP].reshape(GRP * BLK, 2 * W), base)
        copy = forward(base, GROUPS + g)
        copy.start()
        forwards.append(copy)

    take_far(0)
    take_far(1)

    forwards[GROUPS].wait_recv()
    forwards[GROUPS + 1].wait_recv()
    grads(2 * ROWS, 4 * GR, False, False)
    take_far(2)
    forwards[GROUPS + 2].wait_recv()
    grads(2 * ROWS + 4 * GR, 2 * GR, False, False)
    take_far(3)
    forwards[GROUPS + 3].wait_recv()
    grads(2 * ROWS + 6 * GR, 2 * GR, False, True)

    part = ret.at[pl.ds(1, E - 1)]
    pltpu.make_async_copy(part, part, ret_sem).wait()
    for copy in stores:
        copy.wait()
    for copy in forwards:
        copy.wait_send()
    part = packed.at[pl.ds(1, E - 1)]
    pltpu.make_async_copy(part, part, near_send).wait()
    pltpu.make_async_copy(packed, packed, far_send).wait()
    part = back.at[pl.ds(1, E - 1)]
    pltpu.make_async_copy(part, part, ret_send).wait()


def deliver(
    ret_hbm, gin_hbm, gout_hbm, gate_hbm, exp_hbm, slot_hbm,
    dtok_out, dgate_out, gin_out, gout_out,
    ret, gin, gout, gate_ref, exp_ref, slot_ref, dtok, dgate, in_sem, out_sem,
):
    ex = lax.axis_index("expert")
    pairs = (
        (exp_hbm, exp_ref), (slot_hbm, slot_ref), (gate_hbm, gate_ref),
        (ret_hbm, ret), (gin_hbm, gin), (gout_hbm, gout),
    )
    loads = [pltpu.make_async_copy(a, b, in_sem.at[i]) for i, (a, b) in enumerate(pairs)]
    pairs = ((gin, gin_out), (gout, gout_out), (dtok, dtok_out), (dgate, dgate_out))
    stores = [pltpu.make_async_copy(a, b, out_sem.at[i]) for i, (a, b) in enumerate(pairs)]
    for load in loads:
        load.start()
    for load in loads[:3]:
        load.wait()
    slot = slot_ref[...]
    kept = slot >= 0
    relative = (exp_ref[...] - ex + E) & (E - 1)
    code = column(jnp.where(kept, relative * BLK, -4096).astype(F32)).astype(I32)
    slot_column = column(slot.astype(F32)).astype(I32)
    place = iota((T, E * BLK), 1) - code
    hots = [ones_where(place == slot_column + CAP * k) for k in range(D // W)]
    gate_hot = ones_where(place == BLK - 1)
    for load, store in zip(loads[4:], stores[:2]):
        load.wait()
        store.start()
    loads[3].wait()
    returned = ret[...].reshape(E * BLK, W)
    for k in range(D // W):
        dtok[:, k * W : (k + 1) * W] = nn(hots[k], returned).astype(BF)
    stores[2].start()
    picked = nn(gate_hot, returned)
    lane = iota((T, W), 1)
    picked = jnp.where((lane == slot_column) | (lane == slot_column + 128), picked, 0.0)
    sums = jnp.sum(picked, axis=1, keepdims=True)
    diagonal = iota((T, T), 0) == iota((T, T), 1)
    sums = jnp.sum(jnp.where(diagonal, jnp.broadcast_to(sums, (T, T)), 0.0), axis=0, keepdims=True)
    dgate[...] = sums / gate_ref[...]
    stores[3].start()
    for store in stores:
        store.wait()


def body(tokens, upstream, gate_prob, expert_id, slot_index, segment_id, weight_in, weight_out):
    hbm = pl.BlockSpec(memory_space=pl.ANY)
    dma = pltpu.SemaphoreType.DMA
    shape = jax.ShapeDtypeStruct
    gate_row, expert_row, slot_row = (v.reshape(1, T) for v in (gate_prob, expert_id, slot_index))
    gradient = shape((1, FQ, D), BF)
    returned, grad_in, grad_out = pl.pallas_call(
        kernel,
        out_shape=(shape((E, BLK, W), BF), gradient, gradient),
        in_specs=[hbm] * 8,
        out_specs=(hbm,) * 3,
        scratch_shapes=[
            pltpu.VMEM((T, D), BF),
            pltpu.VMEM((T, D), BF),
            pltpu.VMEM((1, T), F32),
            pltpu.VMEM((1, T), I32),
            pltpu.VMEM((1, T), I32),
            pltpu.VMEM((1, T), I32),
            pltpu.VMEM((FF, D), BF),
            pltpu.VMEM((FF, D), BF),
            pltpu.VMEM((E, BLK, 2 * W), BF),
            pltpu.VMEM((E, BLK, 2 * W), BF),
            pltpu.VMEM((E, BLK, 2 * W), BF),
            pltpu.VMEM((4 * ROWS, 2 * D), BF),
            pltpu.VMEM((E, BLK, W), BF),
            pltpu.VMEM((FQ, D), BF),
            pltpu.VMEM((FQ, D), BF),
            pltpu.VMEM((ROWS, D), F32),
            pltpu.VMEM((ROWS, FC), F32),
            pltpu.VMEM((FQ, D), F32),
            pltpu.VMEM((FQ, D), F32),
            pltpu.VMEM((D // W * GR, GRP * BLK), BF),
            dma((6,)),
            dma((2,)),
            pltpu.SemaphoreType.REGULAR,
            dma,
            dma,
            dma,
            dma((GROUPS,)),
            dma((GROUPS,)),
            dma,
            dma((2 * GROUPS,)),
            dma((2 * GROUPS,)),
            dma((2 * FQ // FC + 1,)),
        ],
        compiler_params=pltpu.CompilerParams(
            collective_id=0, has_side_effects=True, vmem_limit_bytes=LIMIT * 2**20
        ),
    )(tokens, upstream, gate_row, expert_row, slot_row, segment_id, weight_in, weight_out)
    d_tokens, d_gate, grad_in, grad_out = pl.pallas_call(
        deliver,
        out_shape=(shape((T, D), BF), shape((1, T), F32), gradient, gradient),
        in_specs=[hbm] * 6,
        out_specs=(hbm,) * 4,
        scratch_shapes=[
            pltpu.VMEM((E, BLK, W), BF),
            pltpu.VMEM((1, FQ, D), BF),
            pltpu.VMEM((1, FQ, D), BF),
            pltpu.VMEM((1, T), F32),
            pltpu.VMEM((1, T), I32),
            pltpu.VMEM((1, T), I32),
            pltpu.VMEM((T, D), BF),
            pltpu.VMEM((1, T), F32),
            dma((6,)),
            dma((4,)),
        ],
        compiler_params=pltpu.CompilerParams(vmem_limit_bytes=LIMIT * 2**20),
    )(returned, grad_in, grad_out, gate_row, expert_row, slot_row)
    return d_tokens, d_gate.reshape(T), grad_in, grad_out


def solution(mesh):
    in_specs = (
        P(("dp", "expert"), None),
        P(("dp", "expert"), None),
        P(("dp", "expert")),
        P(("dp", "expert")),
        P(("dp", "expert")),
        P(("dp", "expert"), None),
        P("expert", None, None),
        P("expert", None, None),
    )
    out_specs = (
        P(("dp", "expert"), None),
        P(("dp", "expert")),
        P("expert", "dp", None),
        P("expert", "dp", None),
    )
    return jax.shard_map(body, mesh=mesh, in_specs=in_specs, out_specs=out_specs, check_vma=False)
```

```python
import math
from functools import partial

import jax
import jax.numpy as jnp
from jax import lax
from jax.experimental import pallas as pl
from jax.experimental.pallas import tpu as pltpu
from jax.sharding import PartitionSpec as P

SEGS = 4
BF = jnp.bfloat16
F32 = jnp.float32
I32 = jnp.int32
MESH = pl.DeviceIdType.MESH
D = 768
FF = 3072
T = 256
E = 64
CAP = 5
W = 256
ROWS = E * CAP
BLK = 16
GRP = 16
GROUPS = E // GRP
GR = GRP * CAP
FQ = FF // 4
FC = 256
LIMIT = 60
FIRST = 28
PACE = 3


def nn(a, b):
    return lax.dot_general(a, b, (((1,), (0,)), ((), ())), preferred_element_type=F32)


def nt(a, b):
    return lax.dot_general(a, b, (((1,), (1,)), ((), ())), preferred_element_type=F32)


def gelu_pair(v):
    scale = math.sqrt(2.0 / math.pi)
    square = v * v
    t = jnp.tanh(scale * (v + 0.044715 * (square * v)))
    half = 0.5 * (1.0 + t)
    slope = half + 0.5 * v * (1.0 - t * t) * (scale * (1.0 + 0.134145 * square))
    return v * half, slope


def iota(shape, dim):
    return lax.broadcasted_iota(I32, shape, dim)


def ones_where(cond):
    return jnp.where(cond, 1.0, 0.0).astype(BF)


def column(row):
    diagonal = iota((T, T), 0) == iota((T, T), 1)
    return jnp.sum(jnp.where(diagonal, jnp.broadcast_to(row, (T, T)), 0.0), axis=1, keepdims=True)


def kernel(
    tok_hbm, up_hbm, gate_hbm, exp_hbm, slot_hbm, seg_hbm, win_hbm, wout_hbm,
    ret, gin_out, gout_out,
    tok_ref, up_ref, gate_ref, exp_ref, slot_ref, seg_ref, win, wout, packed, near, far, rows, back, gin_ref, gout_ref, acc, gate_acc, gin_acc, gout_acc, unpack,
    in_sem, w_sem, ready, near_send, far_send, ret_send, near_sem, far_sem, ret_sem, fwd_send, fwd_sem, out_sem,
):
    dp = lax.axis_index("dp")
    ex = lax.axis_index("expert")
    half = dp // 2
    core = dp % 2
    zl = ex % 4
    z = 4 * half + zl

    x, y = ex // 16, ex // 4 % 4
    def signal(semaphore, group, expert):
        pl.semaphore_signal(semaphore, inc=1, device_id={"dp": group, "expert": expert}, device_id_type=MESH)

    def signal_ring(semaphore):
        for hop in range(1, 8):
            there = (z + hop) % 8
            signal(semaphore, there // 4 * 2 + core, ex - zl + there % 4)

    barrier = pltpu.get_barrier_semaphore()
    signal(barrier, half * 2 + 1 - core, ex)
    for hop in range(1, 16):
        signal(barrier, dp, (x + hop // 4) % 4 * 16 + (y + hop % 4) % 4 * 4 + zl)
    signal_ring(barrier)
    loads = [
        pltpu.make_async_copy(source, target, in_sem.at[index])
        for index, (source, target) in enumerate(
            (
                (up_hbm, up_ref),
                (tok_hbm, tok_ref),
                (seg_hbm, seg_ref),
                (gate_hbm, gate_ref),
                (exp_hbm, exp_ref),
                (slot_hbm, slot_ref),
            )
        )
    ]
    for load in loads:
        load.start()
    for load in loads:
        load.wait()
    win_copy = pltpu.make_async_copy(win_hbm.at[0], win, w_sem.at[0])
    wout_copy = pltpu.make_async_copy(wout_hbm.at[0], wout, w_sem.at[1])

    seg = seg_ref[...]
    weight = jnp.zeros((1, T), F32)
    for label in range(SEGS):
        same = seg == label
        length = jnp.sum(jnp.where(same, 1.0, 0.0), axis=1, keepdims=True)
        weight = weight + jnp.where(same, T / (SEGS * jnp.maximum(length, 1.0)), 0.0)
    gate = gate_ref[...]
    slot = slot_ref[...]
    kept = slot >= 0
    relative = (exp_ref[...] - ex + E) & (E - 1)
    code = jnp.where(kept, relative * BLK + slot, -4096)
    cotangent = (up_ref[...].astype(F32) * column(weight)).astype(BF)
    d_out = (cotangent.astype(F32) * column(gate)).astype(BF)
    tokens = tok_ref[...]
    pl.semaphore_wait(barrier, 23)
    signal_ring(ready)

    def near_half(step):
        hop = jnp.where(step == 2, 2 + 4 * core, jnp.where(step == 3, 7, step))
        return ((z + hop) % 8) // 4

    def send_near(i, carry):
        e = (ex + i) % E
        there = near_half((e % 4 - zl + 4) % 4)
        pltpu.make_async_remote_copy(
            src_ref=packed.at[i], dst_ref=near.at[i], send_sem=near_send, recv_sem=near_sem.at[i // GRP],
            device_id={"dp": there * 2 + core, "expert": e}, device_id_type=MESH,
        ).start()
        return carry

    def send_far(i, carry):
        e = (ex + i) % E
        there = 1 - near_half((e % 4 - zl + 4) % 4)
        pltpu.make_async_remote_copy(
            src_ref=packed.at[i], dst_ref=far.at[i], send_sem=far_send, recv_sem=far_sem.at[i // GRP],
            device_id={"dp": there * 2 + core, "expert": e}, device_id_type=MESH,
        ).start()
        return carry

    for g in range(GROUPS):
        place = iota((GRP * BLK, T), 0) + g * GRP * BLK
        x_sum = jnp.zeros((GRP * BLK, W), F32)
        c_sum = jnp.zeros((GRP * BLK, W), F32)
        for k in range(D // W):
            hot = ones_where(place - CAP * k == code)
            x_sum = x_sum + nn(hot, tokens[:, k * W : (k + 1) * W])
            c_sum = c_sum + nn(hot, d_out[:, k * W : (k + 1) * W])
        packed[g * GRP : (g + 1) * GRP, :, 0:W] = x_sum.astype(BF).reshape(GRP, BLK, W)
        packed[g * GRP : (g + 1) * GRP, :, W : 2 * W] = c_sum.astype(BF).reshape(GRP, BLK, W)
        if g == 0:
            near[0] = packed[0]
            pl.semaphore_wait(ready, 7)
        lax.fori_loop(max(1, g * GRP), (g + 1) * GRP, send_near, 0)
    win_copy.start()
    wout_copy.start()
    lax.fori_loop(0, FIRST, send_far, 0)

    spot = iota((GR, GRP * BLK), 0)
    spot = spot + 11 * ((spot * 205) >> 10)
    for k in range(D // W):
        unpack[k * GR : (k + 1) * GR, :] = ones_where(iota((GR, GRP * BLK), 1) - CAP * k == spot)

    def take(block, base):
        out = nn(unpack[...], block).astype(BF)
        for k in range(D // W):
            rows[pl.ds(base, GR), k * W : (k + 1) * W] = out[k * GR : (k + 1) * GR, 0:W]
            rows[pl.ds(base, GR), D + k * W : D + (k + 1) * W] = out[k * GR : (k + 1) * GR, W : 2 * W]

    def forward(base, index):
        return pltpu.make_async_remote_copy(
            src_ref=rows.at[pl.ds(base, GR)], dst_ref=rows.at[pl.ds(base, GR)],
            send_sem=fwd_send.at[index], recv_sem=fwd_sem.at[index],
            device_id={"dp": half * 2 + 1 - core, "expert": ex}, device_id_type=MESH,
        )

    forwards = []
    own = pl.multiple_of(core * ROWS, BLK)
    for g in range(GROUPS):
        low = 1 if g == 0 else g * GRP
        part = near.at[pl.ds(low, (g + 1) * GRP - low)]
        pltpu.make_async_copy(part, part, near_sem.at[g]).wait()
        base = pl.multiple_of(own + g * GR, BLK)
        take(near[g * GRP : (g + 1) * GRP].reshape(GRP * BLK, 2 * W), base)
        copy = forward(base, g)
        copy.start()
        forwards.append(copy)

    win_copy.wait()
    wout_copy.wait()
    acc[...] = jnp.zeros_like(acc)
    gate_acc[...] = jnp.zeros_like(gate_acc)

    def near_step(j, carry):
        for extra in range(PACE):
            send_far(FIRST + PACE * j + extra, 0)
        units = pl.ds(pl.multiple_of(j * FC, FC), FC)
        mine = pl.ds(own, ROWS)
        pre = nt(rows[mine, 0:D], win[units, :])
        d_hidden = nt(rows[mine, D : 2 * D], wout[units, :])
        hidden, slope = gelu_pair(pre)
        gate_acc[...] += hidden.astype(BF).astype(F32) * d_hidden
        acc[...] += nn((d_hidden * slope).astype(BF), win[units, :])
        return carry

    lax.fori_loop(0, FF // FC, near_step, 0)

    spot = iota((GRP * BLK, GR), 1)
    source = (spot * 205) >> 10
    put = iota((GRP * BLK, GR), 0)
    lane = iota((GR, W), 1)
    here = iota((GR, W), 0)
    here = here - CAP * ((here * 205) >> 10)
    for g in range(GROUPS):
        sums = jnp.sum(gate_acc[g * GR : (g + 1) * GR, :], axis=1, keepdims=True)
        high = sums.astype(BF).astype(F32)
        parts = jnp.where(lane == here, high, jnp.where(lane == here + 128, sums - high, 0.0)).astype(BF)
        out = nn(ones_where(put == source * BLK + BLK - 1), parts)
        for k in range(D // W):
            hot = ones_where(put == spot + 11 * source + CAP * k)
            out = out + nn(hot, acc[g * GR : (g + 1) * GR, k * W : (k + 1) * W].astype(BF))
        back[g * GRP : (g + 1) * GRP] = out.astype(BF).reshape(GRP, BLK, W)
    kept_block = pltpu.make_async_copy(back.at[0], ret.at[0], out_sem.at[2 * FQ // FC])
    kept_block.start()

    def send_back(i, carry):
        e = (ex - i + E) % E
        step = (zl - e % 4 + 4) % 4
        hop = jnp.where(step == 2, 2 + 4 * core, jnp.where(step == 3, 7, step))
        there = ((z - hop + 8) % 8) // 4
        pltpu.make_async_remote_copy(
            src_ref=back.at[i], dst_ref=ret.at[i], send_sem=ret_send, recv_sem=ret_sem,
            device_id={"dp": there * 2 + core, "expert": e}, device_id_type=MESH,
        ).start()
        return carry

    lax.fori_loop(1, E, send_back, 0)

    stores = [kept_block]

    def grads(base, count, first, last):
        def step(j, carry):
            units = pl.ds(pl.multiple_of(dp * FQ + j * FC, FC), FC)
            out = pl.ds(j * FC if last else pl.multiple_of(j * FC, FC), FC)
            x = rows[base : base + count, 0:D]
            c = rows[base : base + count, D : 2 * D]
            hidden, slope = gelu_pair(nt(win[units, :], x))
            d_pre = (nt(wout[units, :], c) * slope).astype(BF)
            g_in = nn(d_pre, x)
            g_out = nn(hidden.astype(BF), c)
            if not first:
                g_in = g_in + gin_acc[out, :]
                g_out = g_out + gout_acc[out, :]
            if last:
                gin_ref[out, :] = g_in.astype(BF)
                gout_ref[out, :] = g_out.astype(BF)
                for index, (source, target) in enumerate(((gin_ref, gin_out), (gout_ref, gout_out))):
                    copy = pltpu.make_async_copy(
                        source.at[out], target.at[0, out], out_sem.at[2 * j + index]
                    )
                    copy.start()
                    stores.append(copy)
            else:
                gin_acc[out, :] = g_in
                gout_acc[out, :] = g_out
            return carry

        if last:
            for j in range(FQ // FC):
                step(j, 0)
        else:
            lax.fori_loop(0, FQ // FC, step, 0)

    for g in range(GROUPS):
        forwards[g].wait_recv()
    grads(0, 2 * ROWS, True, False)

    def take_far(g):
        part = far.at[pl.ds(g * GRP, GRP)]
        pltpu.make_async_copy(part, part, far_sem.at[g]).wait()
        base = pl.multiple_of(2 * ROWS + 2 * g * GR + core * GR, BLK)
        take(far[g * GRP : (g + 1) * GRP].reshape(GRP * BLK, 2 * W), base)
        copy = forward(base, GROUPS + g)
        copy.start()
        forwards.append(copy)

    take_far(0)
    take_far(1)

    forwards[GROUPS].wait_recv()
    forwards[GROUPS + 1].wait_recv()
    grads(2 * ROWS, 4 * GR, False, False)
    take_far(2)
    forwards[GROUPS + 2].wait_recv()
    grads(2 * ROWS + 4 * GR, 2 * GR, False, False)
    take_far(3)
    forwards[GROUPS + 3].wait_recv()
    grads(2 * ROWS + 6 * GR, 2 * GR, False, True)

    part = ret.at[pl.ds(1, E - 1)]
    pltpu.make_async_copy(part, part, ret_sem).wait()
    for copy in stores:
        copy.wait()
    for copy in forwards:
        copy.wait_send()
    part = packed.at[pl.ds(1, E - 1)]
    pltpu.make_async_copy(part, part, near_send).wait()
    pltpu.make_async_copy(packed, packed, far_send).wait()
    part = back.at[pl.ds(1, E - 1)]
    pltpu.make_async_copy(part, part, ret_send).wait()


def deliver(
    ret_hbm, gin_hbm, gout_hbm, gate_hbm, exp_hbm, slot_hbm,
    dtok_out, dgate_out, gin_out, gout_out,
    ret, gin, gout, gate_ref, exp_ref, slot_ref, dtok, dgate, in_sem, out_sem,
):
    ex = lax.axis_index("expert")
    pairs = (
        (exp_hbm, exp_ref), (slot_hbm, slot_ref), (gate_hbm, gate_ref),
        (ret_hbm, ret), (gin_hbm, gin), (gout_hbm, gout),
    )
    loads = [pltpu.make_async_copy(a, b, in_sem.at[i]) for i, (a, b) in enumerate(pairs)]
    pairs = ((gin, gin_out), (gout, gout_out), (dtok, dtok_out), (dgate, dgate_out))
    stores = [pltpu.make_async_copy(a, b, out_sem.at[i]) for i, (a, b) in enumerate(pairs)]
    for load in loads:
        load.start()
    for load in loads[:3]:
        load.wait()
    slot = slot_ref[...]
    kept = slot >= 0
    relative = (exp_ref[...] - ex + E) & (E - 1)
    code = column(jnp.where(kept, relative * BLK, -4096).astype(F32)).astype(I32)
    slot_column = column(slot.astype(F32)).astype(I32)
    place = iota((T, E * BLK), 1) - code
    hots = [ones_where(place == slot_column + CAP * k) for k in range(D // W)]
    gate_hot = ones_where(iota((T, E), 1) * BLK == code)
    for load, store in zip(loads[4:], stores[:2]):
        load.wait()
        store.start()
    loads[3].wait()
    returned = ret[...].reshape(E * BLK, W)
    for k in range(D // W):
        dtok[:, k * W : (k + 1) * W] = nn(hots[k], returned).astype(BF)
    stores[2].start()
    picked = nn(gate_hot, ret[:, BLK - 1, :])
    lane = iota((T, W), 1)
    picked = jnp.where((lane == slot_column) | (lane == slot_column + 128), picked, 0.0)
    sums = jnp.sum(picked, axis=1, keepdims=True)
    diagonal = iota((T, T), 0) == iota((T, T), 1)
    sums = jnp.sum(jnp.where(diagonal, jnp.broadcast_to(sums, (T, T)), 0.0), axis=0, keepdims=True)
    dgate[...] = sums / gate_ref[...]
    stores[3].start()
    for store in stores:
        store.wait()


def body(tokens, upstream, gate_prob, expert_id, slot_index, segment_id, weight_in, weight_out):
    hbm = pl.BlockSpec(memory_space=pl.ANY)
    dma = pltpu.SemaphoreType.DMA
    shape = jax.ShapeDtypeStruct
    gate_row, expert_row, slot_row = (v.reshape(1, T) for v in (gate_prob, expert_id, slot_index))
    gradient = shape((1, FQ, D), BF)
    returned, grad_in, grad_out = pl.pallas_call(
        kernel,
        out_shape=(shape((E, BLK, W), BF), gradient, gradient),
        in_specs=[hbm] * 8,
        out_specs=(hbm,) * 3,
        scratch_shapes=[
            pltpu.VMEM((T, D), BF),
            pltpu.VMEM((T, D), BF),
            pltpu.VMEM((1, T), F32),
            pltpu.VMEM((1, T), I32),
            pltpu.VMEM((1, T), I32),
            pltpu.VMEM((1, T), I32),
            pltpu.VMEM((FF, D), BF),
            pltpu.VMEM((FF, D), BF),
            pltpu.VMEM((E, BLK, 2 * W), BF),
            pltpu.VMEM((E, BLK, 2 * W), BF),
            pltpu.VMEM((E, BLK, 2 * W), BF),
            pltpu.VMEM((4 * ROWS, 2 * D), BF),
            pltpu.VMEM((E, BLK, W), BF),
            pltpu.VMEM((FQ, D), BF),
            pltpu.VMEM((FQ, D), BF),
            pltpu.VMEM((ROWS, D), F32),
            pltpu.VMEM((ROWS, FC), F32),
            pltpu.VMEM((FQ, D), F32),
            pltpu.VMEM((FQ, D), F32),
            pltpu.VMEM((D // W * GR, GRP * BLK), BF),
            dma((6,)),
            dma((2,)),
            pltpu.SemaphoreType.REGULAR,
            dma,
            dma,
            dma,
            dma((GROUPS,)),
            dma((GROUPS,)),
            dma,
            dma((2 * GROUPS,)),
            dma((2 * GROUPS,)),
            dma((2 * FQ // FC + 1,)),
        ],
        compiler_params=pltpu.CompilerParams(
            collective_id=0, has_side_effects=True, vmem_limit_bytes=LIMIT * 2**20
        ),
    )(tokens, upstream, gate_row, expert_row, slot_row, segment_id, weight_in, weight_out)
    d_tokens, d_gate, grad_in, grad_out = pl.pallas_call(
        deliver,
        out_shape=(shape((T, D), BF), shape((1, T), F32), gradient, gradient),
        in_specs=[hbm] * 6,
        out_specs=(hbm,) * 4,
        scratch_shapes=[
            pltpu.VMEM((E, BLK, W), BF),
            pltpu.VMEM((1, FQ, D), BF),
            pltpu.VMEM((1, FQ, D), BF),
            pltpu.VMEM((1, T), F32),
            pltpu.VMEM((1, T), I32),
            pltpu.VMEM((1, T), I32),
            pltpu.VMEM((T, D), BF),
            pltpu.VMEM((1, T), F32),
            dma((6,)),
            dma((4,)),
        ],
        compiler_params=pltpu.CompilerParams(vmem_limit_bytes=LIMIT * 2**20),
    )(returned, grad_in, grad_out, gate_row, expert_row, slot_row)
    return d_tokens, d_gate.reshape(T), grad_in, grad_out


def solution(mesh):
    in_specs = (
        P(("dp", "expert"), None),
        P(("dp", "expert"), None),
        P(("dp", "expert")),
        P(("dp", "expert")),
        P(("dp", "expert")),
        P(("dp", "expert"), None),
        P("expert", None, None),
        P("expert", None, None),
    )
    out_specs = (
        P(("dp", "expert"), None),
        P(("dp", "expert")),
        P("expert", "dp", None),
        P("expert", "dp", None),
    )
    return jax.shard_map(body, mesh=mesh, in_specs=in_specs, out_specs=out_specs, check_vma=False)
```
